32 devices in a mesh: seq: 8 (over z, y), head: 4 (over x, core).
Axes of the slice: x: 2, y: 2, z: 4, core: 2. Of those that a mesh axis runs over, the one named last changes fastest.
Arguments:
- queries: bfloat16 [8192, 4096], P(('seq', 'head')), may hold values from -6 to 6
- key_rows: bfloat16 [8192, 4096], P(('seq', 'head')), may hold values from -6 to 6
- value_rows: bfloat16 [8192, 4096], P(('seq', 'head')), may hold values from -6 to 6
- decay_rates: float32 [32], replicated, as said below
- norm_gain: float32 [4096], replicated, may hold values from 0.5 to 1.5
Outputs:
- attended: bfloat16 [8192, 4096], P(('seq', 'head'))
The draws below stay inside these ranges and needn't reach their ends.
Inputs may be any that keep to these rules, and one draw needn't show every extreme that they name: `decay_rates`: one positive rate per head.
All inputs are finite; a program needn't handle non-finite values.
Results may differ from the reference program's by a relative error of at most 0.003.
Values may be sent and summed in bfloat16 or wider, within the bound.
A program may use at most 512 MiB of HBM per device.

```python
import math
import jax
import jax.numpy as jnp
from jax import lax

HEADS = 32
HEAD_DIM = 128
BLOCK = 256
TOKENS = 8192


def draw_decay_rates(key, part):
    pick_key, slow_key, fast_key = jax.random.split(key, 3)
    keep_share = 0.5
    slow = jnp.exp(jax.random.uniform(slow_key, (HEADS,), jnp.float32, math.log(0.1 / TOKENS), math.log(2.0 / TOKENS)))
    fast = jnp.exp(jax.random.uniform(fast_key, (HEADS,), jnp.float32, math.log(2.0 / TOKENS), math.log(1.0 / 30.0)))
    chosen = jax.random.bernoulli(pick_key, keep_share, (HEADS,))
    return jnp.where(chosen, slow, fast).astype(jnp.float32)


def steps_of(own_key, shape, cuts, low, high):
    gain, own = 1.0, jax.random.fold_in(own_key, 6)
    for dim, shards_of in cuts:
        heights = jnp.exp(jax.random.uniform(jax.random.fold_in(own, dim), (shards_of,), jnp.float32, low / len(cuts), high / len(cuts)))
        gain = gain * jnp.repeat(heights, shape[dim] // shards_of).reshape([-1 if axis == dim else 1 for axis in range(len(shape))])
    return gain


def bell_draw(rng, dims, spread, bound, cuts=(), kind=jnp.bfloat16):
    values = spread * jax.random.normal(rng, dims, jnp.float32)
    if cuts:
        values = values * steps_of(rng, dims, cuts, -0.22, 0.18)
    return jnp.clip(values, -bound, bound).astype(kind)


def setup_inputs(seed: int = 0) -> dict:
    arg_keys = jax.random.split(jax.random.key(seed), 6)
    return {
        "queries": bell_draw(arg_keys[0], (TOKENS, HEADS * HEAD_DIM), 1.0, 6.0, ((0, 32),)),
        "key_rows": bell_draw(arg_keys[1], (TOKENS, HEADS * HEAD_DIM), 1.0, 6.0, ((0, 32),)),
        "value_rows": bell_draw(arg_keys[2], (TOKENS, HEADS * HEAD_DIM), 1.0, 6.0, ((0, 32),)),
        "decay_rates": draw_decay_rates(jax.random.fold_in(arg_keys[5], 71), 0),
        "norm_gain": jnp.clip(1.0 + 0.1 * jax.random.normal(arg_keys[4], (HEADS * HEAD_DIM,), jnp.float32), 0.5, 1.5),
    }


def block_chain(queries, key_rows, value_rows, rates, block):
    tokens, heads, width = queries.shape
    count = tokens // block
    q_blocks = queries.reshape(count, block, heads, width)
    k_blocks = key_rows.reshape(count, block, heads, width)
    v_blocks = value_rows.reshape(count, block, heads, width)
    positions = jnp.arange(block, dtype=jnp.float32)
    offsets = positions[:, None] - positions[None, :]
    within = jnp.where(offsets[None] >= 0.0, jnp.exp(-rates[:, None, None] * jnp.maximum(offsets, 0.0)[None]), 0.0)
    q_decay = jnp.exp(-rates[None, :] * (positions[:, None] + 1.0))[:, :, None]
    k_decay = jnp.exp(-rates[None, :] * (block - 1.0 - positions[:, None]))[:, :, None]
    carry_decay = jnp.exp(-rates * block)[:, None, None]

    def advance(state, items):
        q_part, k_part, v_part = items
        q_wide = q_part.astype(jnp.float32)
        v_wide = v_part.astype(jnp.float32)
        scores = jnp.einsum('ihe,jhe->hij', q_wide, k_part.astype(jnp.float32))
        weights = (scores * within).astype(jnp.bfloat16)
        intra = jnp.einsum('hij,jhe->ihe', weights.astype(jnp.float32), v_wide)
        inter = jnp.einsum('ihe,hef->ihf', q_wide * q_decay, state, precision=lax.Precision.HIGHEST)
        added = jnp.einsum('jhe,jhf->hef', k_part.astype(jnp.float32) * k_decay, v_wide, precision=lax.Precision.HIGHEST)
        return (carry_decay * state + added, intra + inter)
    start = jnp.zeros((heads, width, width), jnp.float32)
    state, outputs = lax.scan(advance, start, (q_blocks, k_blocks, v_blocks))
    return (outputs.reshape(tokens, heads, width), state)

def reference(queries, key_rows, value_rows, decay_rates, norm_gain):
    shaped = (TOKENS, HEADS, HEAD_DIM)
    total, final_state = block_chain(queries.reshape(shaped), key_rows.reshape(shaped), value_rows.reshape(shaped), decay_rates, BLOCK)
    mean_square = lax.optimization_barrier(jnp.mean(total * total, axis=-1, keepdims=True))
    normed = total * lax.rsqrt(mean_square + 1e-06) * norm_gain.reshape(HEADS, HEAD_DIM)
    return normed.astype(jnp.bfloat16).reshape(TOKENS, HEADS * HEAD_DIM)
```

```python
import functools
import jax
import jax.numpy as jnp
from jax import lax
from jax.experimental import pallas as pl
from jax.experimental.pallas import tpu as pltpu
from jax.sharding import PartitionSpec as P

HEADS = 32
HEAD_DIM = 128
BLOCK = 256
CHUNKS = 4
PER_SLOT = 4
F32 = jnp.float32
BF16 = jnp.bfloat16


def split_two(x):
    high = x.astype(BF16)
    low = (x - high.astype(F32)).astype(BF16)
    return jnp.concatenate([high, low], axis=1)


def kernel(
    levels, minor, q_hbm, k_hbm, v_hbm, rates, gains, out_hbm,
    q_ref, k_ref, v_ref, o_ref, total, aggs, lefts, ups, states, downs,
    in_sem, out_sem, up_send, up_recv, dn_send, dn_recv,
):
    heads = HEADS // CHUNKS
    rows = heads * HEAD_DIM
    width = heads * HEAD_DIM
    here = lax.axis_index("seq") * minor + lax.axis_index("head")
    bits = [(here // (1 << k)) % 2 for k in range(levels)]
    partners = []
    for k in range(levels):
        other = here + (1 - 2 * bits[k]) * (1 << k)
        partners.append((other // minor, other % minor))
    starts = [0]
    for k in range(levels - 1):
        starts.append(starts[k] + bits[k] * (rows >> (k + 1)))

    barrier = pltpu.get_barrier_semaphore()
    for partner in partners:
        pl.semaphore_signal(barrier, inc=1, device_id=partner, device_id_type=pl.DeviceIdType.MESH)

    def load(i, c):
        cols = pl.ds(c * width, width)
        src, dst = ((k_hbm, k_ref), (v_hbm, v_ref), (q_hbm, q_ref))[i]
        return pltpu.make_async_copy(src.at[:, cols], dst.at[:, cols], in_sem.at[i, c])

    def save(c):
        cols = pl.ds(c * width, width)
        return pltpu.make_async_copy(o_ref.at[:, cols], out_hbm.at[:, cols], out_sem.at[c])

    for c in range(CHUNKS):
        load(0, c).start()
        load(1, c).start()
    for c in range(CHUNKS):
        load(2, c).start()

    def up_copy(k, c):
        half = rows >> (k + 1)
        if k == levels - 1:
            src = aggs[k].at[c]
        else:
            src = aggs[k].at[c, pl.ds(pl.multiple_of((1 - bits[k]) * half, 8), half)]
        return pltpu.make_async_remote_copy(
            src_ref=src, dst_ref=ups[k].at[c],
            send_sem=up_send.at[k, c], recv_sem=up_recv.at[k, c],
            device_id=partners[k], device_id_type=pl.DeviceIdType.MESH,
        )

    def down_copy(k, c):
        half = rows >> (k + 1)
        spot = pl.ds(pl.multiple_of(bits[k] * half, 8), half)
        return pltpu.make_async_remote_copy(
            src_ref=downs[k].at[c], dst_ref=states[k].at[c, spot],
            send_sem=dn_send.at[k, c], recv_sem=dn_recv.at[k, c],
            device_id=partners[k], device_id_type=pl.DeviceIdType.MESH,
        )

    def head_cols(h):
        return pl.ds(pl.multiple_of(h * HEAD_DIM, HEAD_DIM), HEAD_DIM)

    positions = lax.broadcasted_iota(jnp.int32, (BLOCK, HEAD_DIM), 0).astype(F32)

    def local_states(c):
        def one(i, _):
            h = c * heads + i
            cols = head_cols(h)
            decay = jnp.exp(-rates[h] * (BLOCK - 1.0 - positions))
            wide = split_two(v_ref[:, cols].astype(F32) * decay)
            both = lax.dot_general(
                k_ref[:, cols], wide, (((0,), (0,)), ((), ())), preferred_element_type=F32
            )
            aggs[0][c, pl.ds(pl.multiple_of(i * HEAD_DIM, HEAD_DIM), HEAD_DIM), :] = (
                both[:, :HEAD_DIM] + both[:, HEAD_DIM:]
            )
            return 0

        lax.fori_loop(0, heads, one, 0, unroll=2)

    def segments(k, c):
        half = rows >> (k + 1)
        size = min(half, HEAD_DIM)
        for i in range(half // size):
            head = c * heads + (starts[k + 1] + i * size) // HEAD_DIM
            span = float(BLOCK << k)
            decay = jnp.exp(jnp.full((1, HEAD_DIM), -rates[head] * span, F32))
            yield i * size, size, decay

    def merge_up(k, c):
        half = rows >> (k + 1)
        left = bits[k] == 0
        for at, size, decay in segments(k, c):
            own = aggs[k][c, pl.ds(pl.multiple_of(bits[k] * half + at, 8), size), :]
            got = ups[k][c, pl.ds(at, size), :]
            first = jnp.where(left, own, got)
            second = jnp.where(left, got, own)
            lefts[k][c, pl.ds(at, size), :] = first
            aggs[k + 1][c, pl.ds(at, size), :] = decay * first + second

    def split_down(k, c):
        half = rows >> (k + 1)
        left = bits[k] == 0
        for at, size, decay in segments(k, c):
            before = states[k + 1][c, pl.ds(at, size), :]
            after = decay * before + lefts[k][c, pl.ds(at, size), :]
            states[k][c, pl.ds(pl.multiple_of(bits[k] * half + at, 8), size), :] = jnp.where(
                left, before, after
            )
            downs[k][c, pl.ds(at, size), :] = jnp.where(left, after, before)

    distance = (
        lax.broadcasted_iota(jnp.int32, (BLOCK, BLOCK), 0)
        - lax.broadcasted_iota(jnp.int32, (BLOCK, BLOCK), 1)
    )

    def inside(first, count):
        def one(i, _):
            h = first + i
            cols = head_cols(h)
            scores = lax.dot_general(
                q_ref[:, cols], k_ref[:, cols], (((1,), (1,)), ((), ())), preferred_element_type=F32
            )
            steps = jnp.maximum(distance, 0).astype(F32)
            within = jnp.where(distance >= 0, jnp.exp(-rates[h] * steps), 0.0)
            weights = (scores * within).astype(BF16)
            total[:, cols] = jnp.dot(weights, v_ref[:, cols], preferred_element_type=F32)
            return 0

        lax.fori_loop(0, count, one, 0, unroll=2)

    def finish(c):
        def one(i, _):
            h = c * heads + i
            cols = head_cols(h)
            state = states[0][c, pl.ds(pl.multiple_of(i * HEAD_DIM, HEAD_DIM), HEAD_DIM), :]
            both = jnp.dot(q_ref[:, cols], split_two(state), preferred_element_type=F32)
            inter = both[:, :HEAD_DIM] + both[:, HEAD_DIM:]
            decay = jnp.exp(-rates[h] * (positions + 1.0))
            value = total[:, cols] + decay * inter
            mean_square = jnp.mean(value * value, axis=-1, keepdims=True)
            normed = value * lax.rsqrt(mean_square + 1e-06) * gains[:, cols]
            o_ref[:, cols] = normed.astype(BF16)
            return 0

        lax.fori_loop(0, heads, one, 0, unroll=2)

    top = levels - 1

    def event(e, c):
        if e == 0:
            load(0, c).wait()
            load(1, c).wait()
            local_states(c)
            if c == 0:
                pl.semaphore_wait(barrier, levels)
            up_copy(0, c).start()
        elif e <= top:
            up_copy(e - 1, c).wait_recv()
            merge_up(e - 1, c)
            up_copy(e, c).start()
        else:
            k = 2 * top - e
            if k == top - 1:
                up_copy(top, c).wait_recv()
                got = ups[top][c]
                states[top][c] = jnp.where(bits[top] == 1, got, jnp.zeros_like(got))
            else:
                down_copy(k + 1, c).wait_recv()
            if k >= 0:
                split_down(k, c)
                down_copy(k, c).start()
            else:
                finish(c)
                save(c).start()

    last = 2 * top + 1
    done = 0
    for slot in range(last + CHUNKS):
        for c in range(CHUNKS):
            if 0 <= slot - c <= last:
                if slot - c == last:
                    while done < (c + 1) * heads:
                        inside(done, PER_SLOT)
                        done += PER_SLOT
                event(slot - c, c)
        if slot >= 1 and done < HEADS:
            if done % heads == 0:
                load(2, done // heads).wait()
            inside(done, PER_SLOT)
            done += PER_SLOT
    for c in range(CHUNKS):
        for k in range(levels):
            up_copy(k, c).wait_send()
        for k in range(top):
            down_copy(k, c).wait_send()
        save(c).wait()


def body(queries, key_rows, value_rows, decay_rates, norm_gain):
    major, minor = lax.axis_size("seq"), lax.axis_size("head")
    levels = (major * minor).bit_length() - 1
    assert major * minor == 1 << levels and queries.shape[0] == BLOCK
    rows = HEADS // CHUNKS * HEAD_DIM

    def pieces(first, count):
        return [pltpu.VMEM((CHUNKS, rows >> k, HEAD_DIM), F32) for k in range(first, first + count)]

    top = levels - 1
    full = (BLOCK, HEADS * HEAD_DIM)
    anywhere = pl.BlockSpec(memory_space=pl.ANY)
    return pl.pallas_call(
        functools.partial(kernel, levels, minor),
        out_shape=jax.ShapeDtypeStruct(full, BF16),
        in_specs=[
            anywhere, anywhere, anywhere,
            pl.BlockSpec(memory_space=pltpu.SMEM),
            pl.BlockSpec(memory_space=pltpu.VMEM),
        ],
        out_specs=anywhere,
        scratch_shapes=[
            pltpu.VMEM(full, BF16), pltpu.VMEM(full, BF16), pltpu.VMEM(full, BF16),
            pltpu.VMEM(full, BF16), pltpu.VMEM(full, F32),
            pieces(0, levels),
            pieces(1, top),
            pieces(1, top) + pieces(top, 1),
            pieces(0, levels),
            pieces(1, top),
            pltpu.SemaphoreType.DMA((3, CHUNKS)),
            pltpu.SemaphoreType.DMA((CHUNKS,)),
            pltpu.SemaphoreType.DMA((levels, CHUNKS)),
            pltpu.SemaphoreType.DMA((levels, CHUNKS)),
            pltpu.SemaphoreType.DMA((top, CHUNKS)),
            pltpu.SemaphoreType.DMA((top, CHUNKS)),
        ],
        compiler_params=pltpu.CompilerParams(
            collective_id=0, has_side_effects=True, vmem_limit_bytes=48 << 20
        ),
        cost_estimate=pl.CostEstimate(flops=2 << 30, bytes_accessed=8 << 20, transcendentals=4 << 20),
    )(queries, key_rows, value_rows, decay_rates, norm_gain.reshape(1, HEADS * HEAD_DIM))


def solution(mesh):
    tokens = P(("seq", "head"), None)
    return jax.shard_map(
        body,
        mesh=mesh,
        in_specs=(tokens, tokens, tokens, P(), P()),
        out_specs=tokens,
        check_vma=False,
    )
```

```python
import functools
import jax
import jax.numpy as jnp
from jax import lax
from jax.experimental import pallas as pl
from jax.experimental.pallas import tpu as pltpu
from jax.sharding import PartitionSpec as P

HEADS = 32
HEAD_DIM = 128
BLOCK = 256
CHUNKS = 8
PER_SLOT = 2
RATE_NEAR, RATE_FAR = 300e3, 50e3
DELAY, INSIDE_COST = 1.6, 0.2
F32 = jnp.float32
BF16 = jnp.bfloat16


def split_two(x):
    high = x.astype(BF16)
    low = (x - high.astype(F32)).astype(BF16)
    return jnp.concatenate([high, low], axis=1)


def plan(levels):
    top = levels - 1
    last = 2 * top + 1
    rate = [RATE_NEAR] + [RATE_FAR] * top
    volume = HEADS // CHUNKS * HEAD_DIM * HEAD_DIM * 4
    step, ready = [0] * CHUNKS, [0.0] * CHUNKS
    free = [0.0] * levels
    now, inside_done, order = 0.0, 0, []
    while min(step) <= last:
        open_chunks = [c for c in range(CHUNKS) if step[c] <= last]
        able = [c for c in open_chunks if ready[c] <= now]
        early = [c for c in able if step[c] < last]
        if not early and inside_done < HEADS:
            order.append(("inside", inside_done))
            inside_done += PER_SLOT
            now += INSIDE_COST * PER_SLOT
            continue
        if not able:
            now = min(ready[c] for c in open_chunks)
            continue
        c = max(early or able, key=lambda c: (step[c], -c))
        e = step[c]
        order.append((e, c))
        now += (4.0 if e in (0, last) else 0.6) / CHUNKS + 0.1
        step[c] += 1
        if e < last:
            k = e if e <= top else 2 * top - e
            sent = volume >> (top if e == top else k + 1)
            begin = max(now, free[k])
            free[k] = begin + sent / rate[k]
            ready[c] = free[k] + DELAY
    return order


def kernel(
    levels, minor, q_hbm, k_hbm, v_hbm, rates, gains, out_hbm,
    q_ref, k_ref, v_ref, o_ref, total, aggs, lefts, ups, states, downs,
    in_sem, out_sem, up_send, up_recv, dn_send, dn_recv,
):
    heads = HEADS // CHUNKS
    rows = heads * HEAD_DIM
    width = heads * HEAD_DIM
    here = lax.axis_index("seq") * minor + lax.axis_index("head")
    bits = [(here // (1 << k)) % 2 for k in range(levels)]
    partners = []
    for k in range(levels):
        other = here + (1 - 2 * bits[k]) * (1 << k)
        partners.append((other // minor, other % minor))
    starts = [0]
    for k in range(levels - 1):
        starts.append(starts[k] + bits[k] * (rows >> (k + 1)))

    barrier = pltpu.get_barrier_semaphore()
    for partner in partners:
        pl.semaphore_signal(barrier, inc=1, device_id=partner, device_id_type=pl.DeviceIdType.MESH)

    def load(i, c):
        cols = pl.ds(c * width, width)
        src, dst = ((k_hbm, k_ref), (v_hbm, v_ref), (q_hbm, q_ref))[i]
        return pltpu.make_async_copy(src.at[:, cols], dst.at[:, cols], in_sem.at[i, c])

    def save(c):
        cols = pl.ds(c * width, width)
        return pltpu.make_async_copy(o_ref.at[:, cols], out_hbm.at[:, cols], out_sem.at[c])

    for c in range(CHUNKS):
        load(0, c).start()
        load(1, c).start()
    for c in range(CHUNKS):
        load(2, c).start()

    def up_copy(k, c):
        half = rows >> (k + 1)
        if k == levels - 1:
            src = aggs[k].at[c]
        else:
            src = aggs[k].at[c, pl.ds(pl.multiple_of((1 - bits[k]) * half, 8), half)]
        return pltpu.make_async_remote_copy(
            src_ref=src, dst_ref=ups[k].at[c],
            send_sem=up_send.at[k, c], recv_sem=up_recv.at[k, c],
            device_id=partners[k], device_id_type=pl.DeviceIdType.MESH,
        )

    def down_copy(k, c):
        half = rows >> (k + 1)
        spot = pl.ds(pl.multiple_of(bits[k] * half, 8), half)
        return pltpu.make_async_remote_copy(
            src_ref=downs[k].at[c], dst_ref=states[k].at[c, spot],
            send_sem=dn_send.at[k, c], recv_sem=dn_recv.at[k, c],
            device_id=partners[k], device_id_type=pl.DeviceIdType.MESH,
        )

    def head_cols(h):
        return pl.ds(pl.multiple_of(h * HEAD_DIM, HEAD_DIM), HEAD_DIM)

    positions = lax.broadcasted_iota(jnp.int32, (BLOCK, HEAD_DIM), 0).astype(F32)

    def local_states(c):
        def one(i, _):
            h = c * heads + i
            cols = head_cols(h)
            decay = jnp.exp(-rates[h] * (BLOCK - 1.0 - positions))
            wide = split_two(v_ref[:, cols].astype(F32) * decay)
            both = lax.dot_general(
                k_ref[:, cols], wide, (((0,), (0,)), ((), ())), preferred_element_type=F32
            )
            aggs[0][c, pl.ds(pl.multiple_of(i * HEAD_DIM, HEAD_DIM), HEAD_DIM), :] = (
                both[:, :HEAD_DIM] + both[:, HEAD_DIM:]
            )
            return 0

        lax.fori_loop(0, heads, one, 0, unroll=4)

    def segments(k, c):
        half = rows >> (k + 1)
        size = min(half, HEAD_DIM)
        for i in range(half // size):
            head = c * heads + (starts[k + 1] + i * size) // HEAD_DIM
            span = float(BLOCK << k)
            decay = jnp.exp(jnp.full((1, HEAD_DIM), -rates[head] * span, F32))
            yield i * size, size, decay

    def merge_up(k, c):
        half = rows >> (k + 1)
        left = bits[k] == 0
        for at, size, decay in segments(k, c):
            own = aggs[k][c, pl.ds(pl.multiple_of(bits[k] * half + at, 8), size), :]
            got = ups[k][c, pl.ds(at, size), :]
            first = jnp.where(left, own, got)
            second = jnp.where(left, got, own)
            lefts[k][c, pl.ds(at, size), :] = first
            aggs[k + 1][c, pl.ds(at, size), :] = decay * first + second

    def split_down(k, c):
        half = rows >> (k + 1)
        left = bits[k] == 0
        for at, size, decay in segments(k, c):
            before = states[k + 1][c, pl.ds(at, size), :]
            after = decay * before + lefts[k][c, pl.ds(at, size), :]
            states[k][c, pl.ds(pl.multiple_of(bits[k] * half + at, 8), size), :] = jnp.where(
                left, before, after
            )
            downs[k][c, pl.ds(at, size), :] = jnp.where(left, after, before)

    distance = (
        lax.broadcasted_iota(jnp.int32, (BLOCK, BLOCK), 0)
        - lax.broadcasted_iota(jnp.int32, (BLOCK, BLOCK), 1)
    )

    def inside(first, count):
        def one(i, _):
            h = first + i
            cols = head_cols(h)
            scores = lax.dot_general(
                q_ref[:, cols], k_ref[:, cols], (((1,), (1,)), ((), ())), preferred_element_type=F32
            )
            steps = jnp.maximum(distance, 0).astype(F32)
            within = jnp.where(distance >= 0, jnp.exp(-rates[h] * steps), 0.0)
            weights = (scores * within).astype(BF16)
            total[:, cols] = jnp.dot(weights, v_ref[:, cols], preferred_element_type=F32)
            return 0

        lax.fori_loop(0, count, one, 0, unroll=PER_SLOT)

    def finish(c):
        def one(i, _):
            h = c * heads + i
            cols = head_cols(h)
            state = states[0][c, pl.ds(pl.multiple_of(i * HEAD_DIM, HEAD_DIM), HEAD_DIM), :]
            both = jnp.dot(q_ref[:, cols], split_two(state), preferred_element_type=F32)
            inter = both[:, :HEAD_DIM] + both[:, HEAD_DIM:]
            decay = jnp.exp(-rates[h] * (positions + 1.0))
            value = total[:, cols] + decay * inter
            mean_square = jnp.mean(value * value, axis=-1, keepdims=True)
            normed = value * lax.rsqrt(mean_square + 1e-06) * gains[:, cols]
            o_ref[:, cols] = normed.astype(BF16)
            return 0

        lax.fori_loop(0, heads, one, 0, unroll=4)

    top = levels - 1

    def event(e, c):
        if e == 0:
            load(0, c).wait()
            load(1, c).wait()
            local_states(c)
            if c == 0:
                pl.semaphore_wait(barrier, levels)
            up_copy(0, c).start()
        elif e <= top:
            up_copy(e - 1, c).wait_recv()
            merge_up(e - 1, c)
            up_copy(e, c).start()
        else:
            k = 2 * top - e
            if k == top - 1:
                up_copy(top, c).wait_recv()
                got = ups[top][c]
                states[top][c] = jnp.where(bits[top] == 1, got, jnp.zeros_like(got))
            else:
                down_copy(k + 1, c).wait_recv()
            if k >= 0:
                split_down(k, c)
                down_copy(k, c).start()
            else:
                finish(c)
                save(c).start()

    for e, c in plan(levels):
        if e == "inside":
            if c % heads == 0:
                load(2, c // heads).wait()
            inside(c, PER_SLOT)
        else:
            event(e, c)
    for c in range(CHUNKS):
        for k in range(levels):
            up_copy(k, c).wait_send()
        for k in range(top):
            down_copy(k, c).wait_send()
        save(c).wait()


def body(queries, key_rows, value_rows, decay_rates, norm_gain):
    major, minor = lax.axis_size("seq"), lax.axis_size("head")
    levels = (major * minor).bit_length() - 1
    assert major * minor == 1 << levels and queries.shape[0] == BLOCK
    rows = HEADS // CHUNKS * HEAD_DIM

    def pieces(first, count):
        return [pltpu.VMEM((CHUNKS, rows >> k, HEAD_DIM), F32) for k in range(first, first + count)]

    top = levels - 1
    full = (BLOCK, HEADS * HEAD_DIM)
    anywhere = pl.BlockSpec(memory_space=pl.ANY)
    return pl.pallas_call(
        functools.partial(kernel, levels, minor),
        out_shape=jax.ShapeDtypeStruct(full, BF16),
        in_specs=[
            anywhere, anywhere, anywhere,
            pl.BlockSpec(memory_space=pltpu.SMEM),
            pl.BlockSpec(memory_space=pltpu.VMEM),
        ],
        out_specs=anywhere,
        scratch_shapes=[
            pltpu.VMEM(full, BF16), pltpu.VMEM(full, BF16), pltpu.VMEM(full, BF16),
            pltpu.VMEM(full, BF16), pltpu.VMEM(full, F32),
            pieces(0, levels),
            pieces(1, top),
            pieces(1, top) + pieces(top, 1),
            pieces(0, levels),
            pieces(1, top),
            pltpu.SemaphoreType.DMA((3, CHUNKS)),
            pltpu.SemaphoreType.DMA((CHUNKS,)),
            pltpu.SemaphoreType.DMA((levels, CHUNKS)),
            pltpu.SemaphoreType.DMA((levels, CHUNKS)),
            pltpu.SemaphoreType.DMA((top, CHUNKS)),
            pltpu.SemaphoreType.DMA((top, CHUNKS)),
        ],
        compiler_params=pltpu.CompilerParams(
            collective_id=0, has_side_effects=True, vmem_limit_bytes=62 << 20
        ),
        cost_estimate=pl.CostEstimate(flops=2 << 30, bytes_accessed=8 << 20, transcendentals=4 << 20),
    )(queries, key_rows, value_rows, decay_rates, norm_gain.reshape(1, HEADS * HEAD_DIM))


def solution(mesh):
    tokens = P(("seq", "head"), None)
    return jax.shard_map(
        body,
        mesh=mesh,
        in_specs=(tokens, tokens, tokens, P(), P()),
        out_specs=tokens,
        check_vma=False,
    )
```
